32 devices in a mesh: lon: 8 (over z, y), lat: 4 (over x, core).
Axes of the slice: x: 2, y: 2, z: 4, core: 2. Of those that a mesh axis runs over, the one named last changes fastest.
Arguments:
- heat_anomaly: float32 [75, 32, 1024], P(None, 'lat', 'lon'), may hold values from -6 to 6
- saltiness_anomaly: float32 [75, 32, 1024], P(None, 'lat', 'lon'), may hold values from -6 to 6
- zonal_edge_current: float32 [75, 32, 1024], P(None, 'lat', 'lon'), may hold values from -3 to 3
- meridional_edge_current: float32 [75, 32, 1024], P(None, 'lat', 'lon'), may hold values from -3 to 3
- interface_mixing_coefficient: float32 [74, 32, 1024], P(None, 'lat', 'lon'), may hold values from 0.05 to 5
- ocean_layer_number: int32 [32, 1024], P('lat', 'lon'), may hold values from 0 to 75, as said below
Outputs:
- heat_next: float32 [75, 32, 1024], P(None, 'lat', 'lon')
- saltiness_next: float32 [75, 32, 1024], P(None, 'lat', 'lon')
- zonal_current_next: float32 [75, 32, 1024], P(None, 'lat', 'lon')
- meridional_current_next: float32 [75, 32, 1024], P(None, 'lat', 'lon')
The draws below stay inside these ranges and needn't reach their ends.
Inputs may be any that keep to these rules, and one draw needn't show every extreme that they name: `ocean_layer_number`: 0 marks a land column.
All inputs are finite; a program needn't handle non-finite values.
Results may differ from the reference program's by a relative error of at most 0.0003.
Values sent between devices are 32-bit elements; how exact they have to be, the bound alone decides.
A program may use at most 64 MiB of HBM per device.

```python
import math
import jax
import jax.numpy as jnp

SEA_LAYERS = 75
PARALLEL_POINTS = 1024
MERIDIAN_POINTS = 32


def draw_ocean_layer_number(key, part):
    subkeys = jax.random.split(key, 4)
    block_rows = (MERIDIAN_POINTS - 1) // 4 + 1
    block_cols = (PARALLEL_POINTS - 1) // 32 + 1
    block_depth = jax.random.randint(subkeys[0], (block_rows, block_cols), -(SEA_LAYERS // 2), SEA_LAYERS + SEA_LAYERS // 2)
    deep_row = jax.random.randint(subkeys[1], (), 0, block_rows)
    deep_col = jax.random.randint(subkeys[2], (), 0, block_cols)
    row_ids = jnp.arange(block_rows)[:, None]
    col_ids = jnp.arange(block_cols)[None, :]
    block_depth = jnp.where((row_ids == deep_row) & (col_ids == deep_col), SEA_LAYERS + 20, block_depth)
    block_depth = jnp.where((row_ids == deep_row) & (col_ids == (deep_col + 1) % block_cols), -SEA_LAYERS, block_depth)
    jitter = jax.random.randint(subkeys[3], (MERIDIAN_POINTS, PARALLEL_POINTS), -6, 7)
    column_depth = block_depth[jnp.arange(MERIDIAN_POINTS) // 4][:, jnp.arange(PARALLEL_POINTS) // 32]
    return jnp.clip(column_depth + jitter, 0, SEA_LAYERS).astype(jnp.int32)


def shard_levels(key, extent, cuts, low, high):
    loudness, own = 1.0, jax.random.fold_in(key, 6)
    for position, blocks in cuts:
        steps = jnp.exp(jax.random.uniform(jax.random.fold_in(own, position), (blocks,), jnp.float32, low / len(cuts), high / len(cuts)))
        loudness = loudness * jnp.repeat(steps, extent[position] // blocks).reshape([-1 if axis == position else 1 for axis in range(len(extent))])
    return loudness


def normal_values(stream_key, extent, spread, most, pieces=(), kind=jnp.bfloat16):
    gain = shard_levels(stream_key, extent, pieces, -0.22, 0.18) if pieces else 1.0
    drawn = jax.random.normal(stream_key, extent, jnp.float32) * spread * gain
    return jnp.minimum(jnp.maximum(drawn, -most), most).astype(kind)


def setup_inputs(seed: int = 0) -> dict:
    keys = jax.random.split(jax.random.key(seed), 7)
    heat_anomaly = normal_values(keys[0], (SEA_LAYERS, MERIDIAN_POINTS, PARALLEL_POINTS), 1.0, 6.0, ((1, 4), (2, 8)), jnp.float32)
    saltiness_anomaly = normal_values(keys[1], (SEA_LAYERS, MERIDIAN_POINTS, PARALLEL_POINTS), 1.0, 6.0, ((1, 4), (2, 8)), jnp.float32)
    zonal_edge_current = normal_values(keys[2], (SEA_LAYERS, MERIDIAN_POINTS, PARALLEL_POINTS), 0.5, 3.0, ((1, 4), (2, 8)), jnp.float32)
    meridional_edge_current = normal_values(keys[3], (SEA_LAYERS, MERIDIAN_POINTS, PARALLEL_POINTS), 0.5, 3.0, ((1, 4), (2, 8)), jnp.float32)
    interface_mixing_coefficient = jnp.clip(jnp.exp(math.log(5.0) - 4.6051702 * jax.random.uniform(keys[4], (SEA_LAYERS - 1, MERIDIAN_POINTS, PARALLEL_POINTS), jnp.float32) ** shard_levels(keys[4], (SEA_LAYERS - 1, MERIDIAN_POINTS, PARALLEL_POINTS), ((1, 4), (2, 8)), -0.2, 0.2)), 0.05, 5.0)
    ocean_layer_number = draw_ocean_layer_number(jax.random.fold_in(keys[6], 71), 0)
    return {"heat_anomaly": heat_anomaly, "saltiness_anomaly": saltiness_anomaly, "zonal_edge_current": zonal_edge_current, "meridional_edge_current": meridional_edge_current, "interface_mixing_coefficient": interface_mixing_coefficient, "ocean_layer_number": ocean_layer_number}


time_step = 0.2
diffusion = 0.5
viscosity = 0.5
vertical_viscosity = 0.5
pressure_coef = 0.05
coriolis_coef = 1.5
thermal_coef = 1.0
thermal_curve = 0.2
haline_coef = 0.8
cabbeling_coef = 0.1


def tendencies(heat_grid_values, salt_field, eastward, northward, depth_field, coriolis):
    layer_number = heat_grid_values.shape[0]
    heights = jnp.arange(layer_number, dtype=jnp.float32)[:, None, None] + 0.5
    ocean = (heights < depth_field[None]).astype(jnp.float32)
    density = ocean * (-thermal_coef * (1.0 + 0.5 * thermal_curve * heat_grid_values) * heat_grid_values
                       + haline_coef * salt_field - cabbeling_coef * heat_grid_values * salt_field)
    pressure = pressure_coef * (jnp.cumsum(density, axis=0) - 0.5 * density)
    east_open = ocean[:, 1:-1, :-1] * ocean[:, 1:-1, 1:]
    north_open = ocean[:, :-1, 1:-1] * ocean[:, 1:, 1:-1]
    ocean_mid = ocean[:, 1:-1, 1:-1]
    stars = []
    for tracer in (heat_grid_values, salt_field):
        flux_east = east_open * (eastward[:, 1:-1, :-1] * 0.5 * (tracer[:, 1:-1, :-1] + tracer[:, 1:-1, 1:])
                                 - diffusion * (tracer[:, 1:-1, 1:] - tracer[:, 1:-1, :-1]))
        flux_north = north_open * (northward[:, :-1, 1:-1] * 0.5 * (tracer[:, :-1, 1:-1] + tracer[:, 1:, 1:-1])
                                   - diffusion * (tracer[:, 1:, 1:-1] - tracer[:, :-1, 1:-1]))
        change = flux_east[:, :, 1:] - flux_east[:, :, :-1] + flux_north[:, 1:, :] - flux_north[:, :-1, :]
        stars.append(ocean_mid * (tracer[:, 1:-1, 1:-1] - time_step * change))
    east_mid = east_open[:, :, 1:]
    north_mid = north_open[:, 1:, :]
    zonal_mid = eastward[:, 1:-1, 1:-1]
    merid_mid = northward[:, 1:-1, 1:-1]
    north_avg = 0.25 * (merid_mid + northward[:, 1:-1, 2:] + northward[:, :-2, 1:-1] + northward[:, :-2, 2:])
    east_avg = 0.25 * (zonal_mid + eastward[:, 1:-1, :-2] + eastward[:, 2:, 1:-1] + eastward[:, 2:, :-2])
    zonal_laplacian = (eastward[:, 1:-1, 2:] + eastward[:, 1:-1, :-2] + eastward[:, 2:, 1:-1]
                       + eastward[:, :-2, 1:-1] - 4.0 * zonal_mid)
    merid_laplacian = (northward[:, 1:-1, 2:] + northward[:, 1:-1, :-2] + northward[:, 2:, 1:-1]
                       + northward[:, :-2, 1:-1] - 4.0 * merid_mid)
    press_mid = pressure[:, 1:-1, 1:-1]
    east_star = east_mid * (zonal_mid + time_step * (coriolis * north_avg - (pressure[:, 1:-1, 2:] - press_mid)
                                                      + viscosity * zonal_laplacian))
    north_star = north_mid * (merid_mid + time_step * (-coriolis * east_avg - (pressure[:, 2:, 1:-1] - press_mid)
                                                       + viscosity * merid_laplacian))
    return stars[0], stars[1], east_star, north_star, ocean_mid, east_mid, north_mid


def banded_thomas_elimination(coupling, source):
    layer_number = source.shape[0]
    upper_prime = []
    source_prime = []
    for level_index in range(layer_number):
        divisor = jnp.ones_like(source[level_index])
        numerator = source[level_index]
        if level_index > 0:
            lower_here = -time_step * coupling[level_index - 1]
            divisor = divisor - lower_here - lower_here * upper_prime[level_index - 1]
            numerator = numerator - lower_here * source_prime[level_index - 1]
        if level_index < layer_number - 1:
            upper_here = -time_step * coupling[level_index]
            divisor = divisor - upper_here
            upper_prime.append(upper_here / divisor)
        else:
            upper_prime.append(jnp.zeros_like(numerator))
        source_prime.append(numerator / divisor)
    solved = [None] * layer_number
    solved[layer_number - 1] = source_prime[layer_number - 1]
    for level_index in range(layer_number - 2, -1, -1):
        solved[level_index] = source_prime[level_index] - upper_prime[level_index] * solved[level_index + 1]
    return jnp.stack(solved, axis=0)


def extend_ghost_margin(field, ghost):
    south = jnp.zeros_like(ghost)
    lat_extended = jnp.concatenate([south[..., None, :], field, ghost[..., None, :]], axis=-2)
    return jnp.concatenate([lat_extended[..., -1:], lat_extended, lat_extended[..., :1]], axis=-1)


def reference(heat_anomaly, saltiness_anomaly, zonal_edge_current, meridional_edge_current, interface_mixing_coefficient, ocean_layer_number):
    depth_plain = ocean_layer_number.astype(jnp.float32)
    heat_grid_values = extend_ghost_margin(heat_anomaly, heat_anomaly[:, -1, ::-1])
    salt_field = extend_ghost_margin(saltiness_anomaly, saltiness_anomaly[:, -1, ::-1])
    eastward = extend_ghost_margin(zonal_edge_current, -jnp.roll(zonal_edge_current[:, -1, ::-1], -1, axis=-1))
    northward = extend_ghost_margin(meridional_edge_current, -meridional_edge_current[:, -1, ::-1])
    depth_field = extend_ghost_margin(depth_plain, depth_plain[-1, ::-1])
    row_centres = jnp.arange(MERIDIAN_POINTS).astype(jnp.float32)
    coriolis = (coriolis_coef * (2.0 * (row_centres + 0.5) / MERIDIAN_POINTS - 1.0))[None, :, None]
    heat_interim_guess, salt_star, east_star, north_star, ocean_mid, east_mid, north_mid = tendencies(
        heat_grid_values, salt_field, eastward, northward, depth_field, coriolis)
    scalar_coupling_coefs = interface_mixing_coefficient * ocean_mid[1:]
    heat_next = banded_thomas_elimination(scalar_coupling_coefs, heat_interim_guess)
    saltiness_next = banded_thomas_elimination(scalar_coupling_coefs, salt_star)
    zonal_current_next = banded_thomas_elimination(vertical_viscosity * east_mid[1:], east_star)
    meridional_current_next = banded_thomas_elimination(vertical_viscosity * north_mid[1:], north_star)
    return heat_next, saltiness_next, zonal_current_next, meridional_current_next
```

```python
import functools

import numpy as np
import jax
import jax.numpy as jnp
from jax import lax
from jax.experimental import pallas as pl
from jax.experimental.pallas import tpu as pltpu
from jax.sharding import PartitionSpec as P

MESH = pl.DeviceIdType.MESH
F32 = jnp.float32

time_step = 0.2
coriolis_coef = 1.5
pressure_coef = 0.05


def exchange_kernel(lon_n, lat_n, t_ref, s_ref, u_ref, v_ref, h_ref,
                    rows_ref, cols_ref, corner_ref,
                    row_send, col_send, row_ss, row_rs, col_ss, col_rs, cor_ss, cor_rs, fold_ss):
    levels, height, width = t_ref.shape
    fields = (t_ref, s_ref, u_ref, v_ref)
    lon = lax.axis_index("lon")
    lat = lax.axis_index("lat")
    east = lax.rem(lon + 1, lon_n)
    west = lax.rem(lon + lon_n - 1, lon_n)
    mirror = lon_n - 1 - lon
    second = lax.rem(2 * lon_n - 2 - lon, lon_n)
    top = lat == lat_n - 1
    has_south = lat > 0
    far = jnp.logical_and(top, second != lon)

    barrier = pltpu.get_barrier_semaphore()

    def greet(lon_to, lat_to):
        pl.semaphore_signal(barrier, inc=1, device_id={"lon": lon_to, "lat": lat_to}, device_id_type=MESH)

    greet(east, lat)
    greet(west, lat)

    @pl.when(has_south)
    def _():
        greet(lon, lat - 1)
        greet(east, lat - 1)

    @pl.when(jnp.logical_not(top))
    def _():
        greet(lon, lat + 1)
        greet(west, lat + 1)

    @pl.when(top)
    def _():
        greet(mirror, lat)

    @pl.when(far)
    def _():
        greet(second, lat)

    depth = h_ref[...].astype(F32)
    for f, ref in enumerate(fields):
        row_send[0, f, :levels, :] = ref[:, 0, :]
        row_send[1, f, :levels, :] = ref[:, height - 1, :]
    row_send[0, 0, levels : levels + 1, :] = depth[:1]
    row_send[1, 0, levels : levels + 1, :] = depth[height - 1 :]
    lane = lax.broadcasted_iota(jnp.int32, (height, width), 1)
    zero = jnp.zeros((height, width), F32)

    def pack(k, packs):
        here = lane == k
        out = []
        for f, ref in enumerate(fields):
            x = ref[k]
            out.append(jnp.where(here, pltpu.roll(x, k + 1, 1), packs[2 * f]))
            out.append(jnp.where(here, pltpu.roll(x, k, 1), packs[2 * f + 1]))
        return tuple(out)

    packs = lax.fori_loop(0, levels, pack, (zero,) * 8, unroll=5)
    for f in range(4):
        for side in range(2):
            tile = packs[2 * f + side]
            if f == 0:
                tile = jnp.where(lane == levels, pltpu.roll(depth, levels + 1 - side, 1), tile)
            col_send[side, f] = tile

    def remote(src, dst, send_sem, recv_sem, lon_to, lat_to):
        return pltpu.make_async_remote_copy(
            src_ref=src, dst_ref=dst, send_sem=send_sem, recv_sem=recv_sem,
            device_id={"lon": lon_to, "lat": lat_to}, device_id_type=MESH)

    to_north = remote(row_send.at[1], rows_ref.at[1], row_ss.at[1], row_rs.at[1], lon, lat + 1)
    to_mirror = remote(row_send.at[1], rows_ref.at[0], row_ss.at[1], row_rs.at[0], mirror, lat)
    to_south = remote(row_send.at[0], rows_ref.at[0], row_ss.at[0], row_rs.at[0], lon, lat - 1)
    to_east = remote(col_send.at[0], cols_ref.at[0], col_ss.at[0], col_rs.at[0], east, lat)
    to_west = remote(col_send.at[1], cols_ref.at[1], col_ss.at[1], col_rs.at[1], west, lat)
    to_south_east = remote(col_send.at[0, 2], corner_ref.at[0], cor_ss.at[0], cor_rs.at[0], east, lat - 1)
    to_north_west = remote(col_send.at[1, 3], corner_ref.at[1], cor_ss.at[1], cor_rs.at[1], west, lat + 1)
    to_second = remote(col_send.at[0, 2], corner_ref.at[0], fold_ss, cor_rs.at[0], second, lat)

    peers = (2 + 2 * has_south.astype(jnp.int32) + 2 * jnp.logical_not(top).astype(jnp.int32)
             + top.astype(jnp.int32) + far.astype(jnp.int32))
    pl.semaphore_wait(barrier, peers)

    @pl.when(top)
    def _():
        to_mirror.start()

    @pl.when(jnp.logical_not(top))
    def _():
        to_north.start()

    @pl.when(has_south)
    def _():
        to_south.start()

    @pl.when(far)
    def _():
        to_second.start()

    @pl.when(jnp.logical_and(top, second == lon))
    def _():
        corner_ref[0] = col_send[0, 2]

    @pl.when(jnp.logical_not(top))
    def _():
        to_north_west.start()

    @pl.when(has_south)
    def _():
        to_south_east.start()

    to_east.start()
    to_west.start()

    to_east.wait()
    to_west.wait()

    @pl.when(has_south)
    def _():
        to_south.wait_send()
        to_south_east.wait_send()
        to_north.wait_recv()
        to_north_west.wait_recv()

    @pl.when(jnp.logical_not(top))
    def _():
        to_north.wait_send()
        to_north_west.wait_send()
        to_south_east.wait_recv()

    @pl.when(top)
    def _():
        to_mirror.wait_send()

    @pl.when(far)
    def _():
        to_second.wait_send()
        to_second.wait_recv()

    to_south.wait_recv()


def face_tables(levels):
    part = time_step * 0.5
    ahead, last, factor = [], [], [0.0]
    for k in range(levels):
        above = part * (1.0 - factor[k]) if k else 0.0
        ahead.append(1.0 / (1.0 + part + above))
        last.append(1.0 / (1.0 + above))
        factor.append(part * ahead[k])
    return [np.asarray(x, np.float32) for x in (ahead, last, factor)]


def at_level(table, k):
    steady = table[-1]
    value = jnp.float32(float(steady))
    for i in range(len(table)):
        if table[i] != steady:
            value = jnp.where(k == i, jnp.float32(float(table[i])), value)
    return value


def column_kernel(lat_n, t_ref, s_ref, u_ref, v_ref, mix_ref, h_ref, rows_ref, cols_ref, corner_ref,
                  to_ref, so_ref, uo_ref, vo_ref, north_ref, south_ref, w_ref):
    levels, height, width = t_ref.shape
    padded = rows_ref.shape[2]
    lat = lax.axis_index("lat")
    top = lat == lat_n - 1
    has_south = lat > 0
    lane = lax.broadcasted_iota(jnp.int32, (height, width), 1)
    row = lax.broadcasted_iota(jnp.int32, (height, width), 0)
    first_lane, last_lane = lane == 0, lane == width - 1
    first_row, last_row = row == 0, row == height - 1
    wide_lane = lax.broadcasted_iota(jnp.int32, (padded, width), 1)

    def lanes(x, index):
        return jnp.take_along_axis(x, index, axis=1)

    plain = jnp.where(top, width - 1 - wide_lane, wide_lane)
    sign = jnp.where(top, -1.0, 1.0).astype(F32)
    corner = jnp.where(top, corner_ref[0, height - 1 :, :], corner_ref[0, :1, :])
    corner = jnp.transpose(jnp.broadcast_to(corner, (width, width)))[:padded]
    north_ref[0] = lanes(rows_ref[0, 0], plain)
    north_ref[1] = lanes(rows_ref[0, 1], plain)
    zonal = lanes(rows_ref[0, 2], plain)
    left = pltpu.roll(zonal, width - 1, 1)
    right = pltpu.roll(zonal, 1, 1)
    here = jnp.where(top, jnp.where(wide_lane == width - 1, corner, left), zonal)
    behind = jnp.where(top, zonal, jnp.where(wide_lane == 0, corner, right))
    north_ref[2] = sign * here
    north_ref[3] = sign * lanes(rows_ref[0, 3], plain)
    north_ref[4] = sign * (here + behind)

    corner = jnp.transpose(jnp.broadcast_to(corner_ref[1, height - 1 :, :], (width, width)))[:padded]
    merid = rows_ref[1, 3]
    for f in range(4):
        south_ref[f] = jnp.where(has_south, rows_ref[1, f], 0.0)
    ahead = jnp.where(wide_lane == width - 1, corner, pltpu.roll(merid, width - 1, 1))
    south_ref[4] = jnp.where(has_south, merid + ahead, 0.0)

    def to_east(x, f, k):
        return jnp.where(last_lane, pltpu.roll(cols_ref[1, f], width - 1 - k, 1), pltpu.roll(x, width - 1, 1))

    def to_west(x, f, k):
        return jnp.where(first_lane, pltpu.roll(cols_ref[0, f], lax.rem(width - k, width), 1), pltpu.roll(x, 1, 1))

    def to_north(x, f, k):
        return jnp.where(last_row, north_ref[f, pl.ds(k, 1), :], pltpu.roll(x, height - 1, 0))

    def to_south(x, f, k):
        return jnp.where(first_row, south_ref[f, pl.ds(k, 1), :], pltpu.roll(x, 1, 0))

    depth = h_ref[...].astype(F32)
    east_depth = jnp.minimum(depth, to_east(depth, 0, levels))
    west_depth = jnp.minimum(depth, to_west(depth, 0, levels))
    north_depth = jnp.minimum(depth, to_north(depth, 0, levels))
    south_depth = jnp.minimum(depth, to_south(depth, 0, levels))

    centre = (lat * height + row).astype(F32) + 0.5
    coriolis = coriolis_coef * (2.0 * centre / (height * lat_n) - 1.0)
    spin = (0.25 * time_step) * coriolis
    tables = face_tables(levels)
    push = time_step * pressure_coef
    part = time_step * 0.5

    def density(t, s):
        return 0.8 * s - t * (1.0 + 0.1 * (t + s))

    def down(k, carry):
        heat, salt, zonal, merid, a, w, east_sum, north_sum = carry
        level = k.astype(F32) + 0.5
        t, s, u, v = t_ref[k], s_ref[k], u_ref[k], v_ref[k]
        te, tw, tn, ts = to_east(t, 0, k), to_west(t, 0, k), to_north(t, 0, k), to_south(t, 0, k)
        se, sw, sn, ss = to_east(s, 1, k), to_west(s, 1, k), to_north(s, 1, k), to_south(s, 1, k)
        ue, uw, un, us = to_east(u, 2, k), to_west(u, 2, k), to_north(u, 2, k), to_south(u, 2, k)
        ve, vw, vn, vs = to_east(v, 3, k), to_west(v, 3, k), to_north(v, 3, k), to_south(v, 3, k)
        uu, vv = u + uw, v + ve
        ubar = uu + to_north(uu, 4, k)
        vbar = vv + to_south(vv, 4, k)
        open_c = level < depth
        open_e, open_w = level < east_depth, level < west_depth
        open_n, open_s = level < north_depth, level < south_depth

        def face(mask, speed):
            x = part * speed
            return jnp.where(mask, part - x, 0.0), jnp.where(mask, part + x, 0.0)

        e_far, e_own = face(open_e, u)
        w_own, w_far = face(open_w, uw)
        n_far, n_own = face(open_n, v)
        s_own, s_far = face(open_s, vs)
        own = 1.0 - e_own - w_own - n_own - s_own
        t_star = own * t + e_far * te + w_far * tw + n_far * tn + s_far * ts
        s_star = own * s + e_far * se + w_far * sw + n_far * sn + s_far * ss

        rho = density(t, s)
        east_step = density(te, se) - rho
        north_step = density(tn, sn) - rho
        half_e = push * 0.5 * east_step
        half_n = push * 0.5 * north_step
        east_push = east_sum + half_e
        north_push = north_sum + half_n
        u_star = (1.0 - 4.0 * part) * u + part * (ue + uw + un + us) + spin * vbar - east_push
        v_star = (1.0 - 4.0 * part) * v + part * (ve + vw + vn + vs) - spin * ubar - north_push

        below = jnp.minimum(k, levels - 2)
        a_next = jnp.where(level + 1.0 < depth, time_step * mix_ref[below], 0.0)
        d = (1.0 + a_next + a) - a * w
        r = pl.reciprocal(d, approx=True)
        r = r * (2.0 - d * r)
        w_next = a_next * r
        heat = jnp.where(open_c, (t_star + a * heat) * r, 0.0)
        salt = jnp.where(open_c, (s_star + a * salt) * r, 0.0)
        r_ahead, r_last = at_level(tables[0], k), at_level(tables[1], k)
        r_e = jnp.where(level + 1.0 < east_depth, r_ahead, r_last)
        r_n = jnp.where(level + 1.0 < north_depth, r_ahead, r_last)
        zonal = jnp.where(open_e, (u_star + part * zonal) * r_e, 0.0)
        merid = jnp.where(open_n, (v_star + part * merid) * r_n, 0.0)
        to_ref[k] = heat
        so_ref[k] = salt
        uo_ref[k] = zonal
        vo_ref[k] = merid
        w_ref[k] = w_next
        return heat, salt, zonal, merid, a_next, w_next, east_push + half_e, north_push + half_n

    zero = jnp.zeros((height, width), F32)
    out = lax.fori_loop(0, levels, down, (zero,) * 8, unroll=3)

    def up(i, carry):
        heat, salt, zonal, merid = carry
        k = levels - 2 - i
        w = w_ref[k]
        wc = at_level(tables[2][1:], k)
        heat = to_ref[k] + w * heat
        salt = so_ref[k] + w * salt
        zonal = uo_ref[k] + wc * zonal
        merid = vo_ref[k] + wc * merid
        to_ref[k] = heat
        so_ref[k] = salt
        uo_ref[k] = zonal
        vo_ref[k] = merid
        return heat, salt, zonal, merid

    lax.fori_loop(0, levels - 1, up, out[:4], unroll=2)


def local(lon_n, lat_n, t, s, u, v, mix, h):
    levels, height, width = t.shape
    padded = (levels + 1 + 7) // 8 * 8
    vmem = pl.BlockSpec(memory_space=pltpu.VMEM)
    shape = functools.partial(jax.ShapeDtypeStruct, dtype=F32)
    dma = pltpu.SemaphoreType.DMA
    rows, cols, corners = pl.pallas_call(
        functools.partial(exchange_kernel, lon_n, lat_n),
        out_shape=(shape((2, 4, padded, width)), shape((2, 4, height, width)), shape((2, height, width))),
        in_specs=[vmem] * 5,
        out_specs=(vmem,) * 3,
        scratch_shapes=[
            pltpu.VMEM((2, 4, padded, width), F32),
            pltpu.VMEM((2, 4, height, width), F32),
            dma((2,)), dma((2,)), dma((2,)), dma((2,)), dma((2,)), dma((2,)), dma,
        ],
        compiler_params=pltpu.CompilerParams(
            collective_id=0, has_side_effects=True, vmem_limit_bytes=16 << 20),
    )(t, s, u, v, h)
    field = shape((levels, height, width))
    return pl.pallas_call(
        functools.partial(column_kernel, lat_n),
        out_shape=(field,) * 4,
        in_specs=[vmem] * 9,
        out_specs=(vmem,) * 4,
        scratch_shapes=[
            pltpu.VMEM((5, padded, width), F32),
            pltpu.VMEM((5, padded, width), F32),
            pltpu.VMEM((levels, height, width), F32),
        ],
        compiler_params=pltpu.CompilerParams(vmem_limit_bytes=32 << 20),
    )(t, s, u, v, mix, h, rows, cols, corners)


def solution(mesh):
    field = P(None, "lat", "lon")
    return jax.shard_map(
        functools.partial(local, mesh.shape["lon"], mesh.shape["lat"]),
        mesh=mesh,
        in_specs=(field,) * 5 + (P("lat", "lon"),),
        out_specs=(field,) * 4,
        check_vma=False,
    )
```

```python
import functools

import numpy as np
import jax
import jax.numpy as jnp
from jax import lax
from jax.experimental import pallas as pl
from jax.experimental.pallas import tpu as pltpu
from jax.sharding import PartitionSpec as P

MESH = pl.DeviceIdType.MESH
F32 = jnp.float32

time_step = 0.2
coriolis_coef = 1.5
pressure_coef = 0.05


def face_tables(levels):
    part = time_step * 0.5
    ahead, last, factor = [], [], [0.0]
    for k in range(levels):
        above = part * (1.0 - factor[k]) if k else 0.0
        ahead.append(1.0 / (1.0 + part + above))
        last.append(1.0 / (1.0 + above))
        factor.append(part * ahead[k])
    return [np.asarray(x, np.float32) for x in (ahead, last, factor)]


def at_level(table, k):
    steady = table[-1]
    value = jnp.float32(float(steady))
    for i in range(len(table)):
        if table[i] != steady:
            value = jnp.where(k == i, jnp.float32(float(table[i])), value)
    return value


def chunks(levels, padded):
    size = padded // 3 // 8 * 8
    starts = [i * size for i in range(3)]
    stops = starts[1:] + [padded]
    return [(a, b, min(b, levels)) for a, b in zip(starts, stops)]


def forward_kernel(lon_n, lat_n, t_hbm, s_hbm, u_hbm, v_hbm, mix_hbm, h_hbm,
                   to_ref, so_ref, uo_ref, vo_ref, w_ref,
                   fields, mix, deep, deep_send, deep_got, row_send, rows, col_send, cols, corners,
                   north_ref, south_ref,
                   in_sem, deep_ss, deep_rs, row_ss, row_rs, col_ss, col_rs, cor_ss, cor_rs, fold_ss):
    levels, height, width = t_hbm.shape
    padded = rows.shape[2]
    parts = chunks(levels, padded)
    lon = lax.axis_index("lon")
    lat = lax.axis_index("lat")
    east = lax.rem(lon + 1, lon_n)
    west = lax.rem(lon + lon_n - 1, lon_n)
    mirror = lon_n - 1 - lon
    second = lax.rem(2 * lon_n - 2 - lon, lon_n)
    top = lat == lat_n - 1
    inner = jnp.logical_not(top)
    has_south = lat > 0
    far = jnp.logical_and(top, second != lon)

    loads = [pltpu.make_async_copy(src, dst, in_sem.at[i]) for i, (src, dst) in enumerate([
        (h_hbm, deep), (t_hbm, fields.at[0]), (s_hbm, fields.at[1]),
        (u_hbm, fields.at[2]), (v_hbm, fields.at[3]), (mix_hbm, mix)])]
    for load in loads:
        load.start()

    barrier = pltpu.get_barrier_semaphore()

    def greet(lon_to, lat_to):
        pl.semaphore_signal(barrier, inc=1, device_id={"lon": lon_to, "lat": lat_to}, device_id_type=MESH)

    @pl.when(top)
    def _():
        greet(mirror, lat)

    @pl.when(far)
    def _():
        greet(second, lat)

    greet(east, lat)
    greet(west, lat)

    @pl.when(has_south)
    def _():
        greet(lon, lat - 1)
        greet(east, lat - 1)

    @pl.when(inner)
    def _():
        greet(lon, lat + 1)
        greet(west, lat + 1)

    def remote(src, dst, send_sem, recv_sem, lon_to, lat_to):
        return pltpu.make_async_remote_copy(
            src_ref=src, dst_ref=dst, send_sem=send_sem, recv_sem=recv_sem,
            device_id={"lon": lon_to, "lat": lat_to}, device_id_type=MESH)

    def row_copy(c, own, slot, lon_to, lat_to):
        a, b, _ = parts[c]
        return remote(row_send.at[own, :, a:b], rows.at[slot, :, a:b], row_ss.at[own, c], row_rs.at[slot, c], lon_to, lat_to)

    to_north = [row_copy(c, 1, 1, lon, lat + 1) for c in range(3)]
    to_mirror = [row_copy(c, 1, 0, mirror, lat) for c in range(3)]
    to_south = [row_copy(c, 0, 0, lon, lat - 1) for c in range(3)]
    to_north.append(remote(deep_send, deep_got.at[1], deep_ss.at[1], deep_rs.at[1], lon, lat + 1))
    to_mirror.append(remote(deep_send, deep_got.at[0], deep_ss.at[1], deep_rs.at[0], mirror, lat))
    to_south.append(remote(deep_send, deep_got.at[0], deep_ss.at[0], deep_rs.at[0], lon, lat - 1))
    to_east = remote(col_send.at[0], cols.at[0], col_ss.at[0], col_rs.at[0], east, lat)
    to_west = remote(col_send.at[1], cols.at[1], col_ss.at[1], col_rs.at[1], west, lat)
    to_south_east = remote(col_send.at[0, 2], corners.at[0], cor_ss.at[0], cor_rs.at[0], east, lat - 1)
    to_north_west = remote(col_send.at[1, 3], corners.at[1], cor_ss.at[1], cor_rs.at[1], west, lat + 1)
    to_second = remote(col_send.at[0, 2], corners.at[0], fold_ss, cor_rs.at[0], second, lat)

    def send_rows(pieces):
        @pl.when(top)
        def _():
            for c in pieces:
                to_mirror[c].start()

        @pl.when(inner)
        def _():
            for c in pieces:
                to_north[c].start()

        @pl.when(has_south)
        def _():
            for c in pieces:
                to_south[c].start()

    loads[0].wait()
    depth = deep[...].astype(F32)
    deep_send[...] = depth
    for f in range(4):
        loads[1 + f].wait()
        row_send[0, f, :levels, :] = fields[f, :, 0, :]
        row_send[1, f, :levels, :] = fields[f, :, height - 1, :]

    peers = (2 + 2 * has_south.astype(jnp.int32) + 2 * inner.astype(jnp.int32)
             + top.astype(jnp.int32) + far.astype(jnp.int32))
    pl.semaphore_wait(barrier, peers)
    send_rows([3, 0])

    lane = lax.broadcasted_iota(jnp.int32, (height, width), 1)
    row = lax.broadcasted_iota(jnp.int32, (height, width), 0)
    zero = jnp.zeros((height, width), F32)

    def pack(k, packs):
        here = lane == k
        out = []
        for f in range(4):
            x = fields[f, k]
            out.append(jnp.where(here, pltpu.roll(x, k + 1, 1), packs[2 * f]))
            out.append(jnp.where(here, pltpu.roll(x, k, 1), packs[2 * f + 1]))
        return tuple(out)

    packs = lax.fori_loop(0, levels, pack, (zero,) * 8, unroll=5)
    for f in range(4):
        for side in range(2):
            tile = packs[2 * f + side]
            if f == 0:
                tile = jnp.where(lane == levels, pltpu.roll(depth, levels + 1 - side, 1), tile)
            col_send[side, f] = tile

    to_east.start()
    to_west.start()

    @pl.when(far)
    def _():
        to_second.start()

    @pl.when(jnp.logical_and(top, second == lon))
    def _():
        corners[0] = col_send[0, 2]

    @pl.when(inner)
    def _():
        to_north_west.start()

    @pl.when(has_south)
    def _():
        to_south_east.start()

    send_rows([1, 2])

    first_lane, last_lane = lane == 0, lane == width - 1
    first_row, last_row = row == 0, row == height - 1

    def lanes(x, index):
        return jnp.take_along_axis(x, index, axis=1)

    def turned(x):
        wide = lax.broadcasted_iota(jnp.int32, x.shape, 1)
        return lanes(x, jnp.where(top, width - 1 - wide, wide))

    sign = jnp.where(top, -1.0, 1.0).astype(F32)
    loads[5].wait()
    to_east.wait()
    to_west.wait()

    @pl.when(inner)
    def _():
        to_south_east.wait_recv()
        to_north_west.wait_send()

    @pl.when(has_south)
    def _():
        to_north_west.wait_recv()
        to_south_east.wait_send()
        to_north[3].wait_recv()

    @pl.when(far)
    def _():
        to_second.wait()

    to_south[3].wait_recv()
    north_deep = turned(jnp.where(top, pltpu.roll(deep_got[0], 1, 0), deep_got[0]))[:1]
    south_deep = jnp.where(has_south, deep_got[1], 0.0)[height - 1 :]
    north_corner = jnp.where(top, corners[0, height - 1 :, :], corners[0, :1, :])
    north_corner = jnp.transpose(jnp.broadcast_to(north_corner, (width, width)))[:padded]
    south_corner = jnp.transpose(jnp.broadcast_to(corners[1, height - 1 :, :], (width, width)))[:padded]

    def take_rows(c):
        a, b, _ = parts[c]
        to_south[c].wait_recv()

        @pl.when(has_south)
        def _():
            to_north[c].wait_recv()

        wide_lane = lax.broadcasted_iota(jnp.int32, (b - a, width), 1)
        corner = north_corner[a:b]
        north_ref[0, a:b] = turned(rows[0, 0, a:b])
        north_ref[1, a:b] = turned(rows[0, 1, a:b])
        zonal = turned(rows[0, 2, a:b])
        left = pltpu.roll(zonal, width - 1, 1)
        right = pltpu.roll(zonal, 1, 1)
        here = jnp.where(top, jnp.where(wide_lane == width - 1, corner, left), zonal)
        behind = jnp.where(top, zonal, jnp.where(wide_lane == 0, corner, right))
        north_ref[2, a:b] = sign * here
        north_ref[3, a:b] = sign * turned(rows[0, 3, a:b])
        north_ref[4, a:b] = sign * (here + behind)
        merid = rows[1, 3, a:b]
        for f in range(4):
            south_ref[f, a:b] = jnp.where(has_south, rows[1, f, a:b], 0.0)
        ahead = jnp.where(wide_lane == width - 1, south_corner[a:b], pltpu.roll(merid, width - 1, 1))
        south_ref[4, a:b] = jnp.where(has_south, merid + ahead, 0.0)

    def to_east_of(x, f, k):
        return jnp.where(last_lane, pltpu.roll(cols[1, f], width - 1 - k, 1), pltpu.roll(x, width - 1, 1))

    def to_west_of(x, f, k):
        return jnp.where(first_lane, pltpu.roll(cols[0, f], lax.rem(width - k, width), 1), pltpu.roll(x, 1, 1))

    def to_north_of(x, f, k):
        return jnp.where(last_row, north_ref[f, pl.ds(k, 1), :], pltpu.roll(x, height - 1, 0))

    def to_south_of(x, f, k):
        return jnp.where(first_row, south_ref[f, pl.ds(k, 1), :], pltpu.roll(x, 1, 0))

    east_depth = jnp.minimum(depth, to_east_of(depth, 0, levels))
    west_depth = jnp.minimum(depth, to_west_of(depth, 0, levels))
    north_depth = jnp.minimum(depth, jnp.where(last_row, north_deep, pltpu.roll(depth, height - 1, 0)))
    south_depth = jnp.minimum(depth, jnp.where(first_row, south_deep, pltpu.roll(depth, 1, 0)))

    centre = (lat * height + row).astype(F32) + 0.5
    coriolis = coriolis_coef * (2.0 * centre / (height * lat_n) - 1.0)
    spin = (0.25 * time_step) * coriolis
    tables = face_tables(levels)
    push = time_step * pressure_coef
    part = time_step * 0.5

    def density(t, s):
        return 0.8 * s - t * (1.0 + 0.1 * (t + s))

    def down(k, carry):
        heat, salt, zonal, merid, a, w, east_sum, north_sum = carry
        level = k.astype(F32) + 0.5
        t, s, u, v = fields[0, k], fields[1, k], fields[2, k], fields[3, k]
        te, tw, tn, ts = to_east_of(t, 0, k), to_west_of(t, 0, k), to_north_of(t, 0, k), to_south_of(t, 0, k)
        se, sw, sn, ss = to_east_of(s, 1, k), to_west_of(s, 1, k), to_north_of(s, 1, k), to_south_of(s, 1, k)
        ue, uw, un, us = to_east_of(u, 2, k), to_west_of(u, 2, k), to_north_of(u, 2, k), to_south_of(u, 2, k)
        ve, vw, vn, vs = to_east_of(v, 3, k), to_west_of(v, 3, k), to_north_of(v, 3, k), to_south_of(v, 3, k)
        uu, vv = u + uw, v + ve
        ubar = uu + to_north_of(uu, 4, k)
        vbar = vv + to_south_of(vv, 4, k)
        open_c = level < depth
        open_e, open_w = level < east_depth, level < west_depth
        open_n, open_s = level < north_depth, level < south_depth

        def face(mask, speed):
            x = part * speed
            return jnp.where(mask, part - x, 0.0), jnp.where(mask, part + x, 0.0)

        e_far, e_own = face(open_e, u)
        w_own, w_far = face(open_w, uw)
        n_far, n_own = face(open_n, v)
        s_own, s_far = face(open_s, vs)
        own = 1.0 - e_own - w_own - n_own - s_own
        t_star = own * t + e_far * te + w_far * tw + n_far * tn + s_far * ts
        s_star = own * s + e_far * se + w_far * sw + n_far * sn + s_far * ss

        rho = density(t, s)
        east_step = density(te, se) - rho
        north_step = density(tn, sn) - rho
        half_e = push * 0.5 * east_step
        half_n = push * 0.5 * north_step
        east_push = east_sum + half_e
        north_push = north_sum + half_n
        u_star = (1.0 - 4.0 * part) * u + part * (ue + uw + un + us) + spin * vbar - east_push
        v_star = (1.0 - 4.0 * part) * v + part * (ve + vw + vn + vs) - spin * ubar - north_push

        below = jnp.minimum(k, levels - 2)
        a_next = jnp.where(level + 1.0 < depth, time_step * mix[below], 0.0)
        d = (1.0 + a_next + a) - a * w
        r = pl.reciprocal(d, approx=True)
        r = r * (2.0 - d * r)
        w_next = a_next * r
        heat = jnp.where(open_c, (t_star + a * heat) * r, 0.0)
        salt = jnp.where(open_c, (s_star + a * salt) * r, 0.0)
        r_ahead, r_last = at_level(tables[0], k), at_level(tables[1], k)
        r_e = jnp.where(level + 1.0 < east_depth, r_ahead, r_last)
        r_n = jnp.where(level + 1.0 < north_depth, r_ahead, r_last)
        zonal = jnp.where(open_e, (u_star + part * zonal) * r_e, 0.0)
        merid = jnp.where(open_n, (v_star + part * merid) * r_n, 0.0)
        to_ref[k] = heat
        so_ref[k] = salt
        uo_ref[k] = zonal
        vo_ref[k] = merid
        w_ref[k] = w_next
        return heat, salt, zonal, merid, a_next, w_next, east_push + half_e, north_push + half_n

    state = (zero,) * 8
    for c in range(3):
        take_rows(c)
        state = lax.fori_loop(parts[c][0], parts[c][2], down, state, unroll=3)

    @pl.when(top)
    def _():
        for copy in to_mirror:
            copy.wait_send()

    @pl.when(inner)
    def _():
        for copy in to_north:
            copy.wait_send()

    @pl.when(has_south)
    def _():
        for copy in to_south:
            copy.wait_send()


def backward_kernel(to_ref, so_ref, uo_ref, vo_ref, w_ref, t_hbm, s_hbm, u_hbm, v_hbm, out, sem):
    levels, height, width = to_ref.shape
    factors = face_tables(levels)[2][1:]
    results = (t_hbm, s_hbm, u_hbm, v_hbm)
    heat, salt, zonal, merid = (ref[levels - 1] for ref in (to_ref, so_ref, uo_ref, vo_ref))
    for f, x in enumerate((heat, salt, zonal, merid)):
        out[f, levels - 1] = x

    def up(i, carry):
        heat, salt, zonal, merid = carry
        k = levels - 1 - i
        w = w_ref[k]
        wc = at_level(factors, k)
        heat = to_ref[k] + w * heat
        salt = so_ref[k] + w * salt
        zonal = uo_ref[k] + wc * zonal
        merid = vo_ref[k] + wc * merid
        for f, x in enumerate((heat, salt, zonal, merid)):
            out[f, k] = x
        return heat, salt, zonal, merid

    state = (heat, salt, zonal, merid)
    pieces = 4
    bounds = [levels * i // pieces for i in range(pieces + 1)]
    copies = []
    for i in range(pieces):
        state = lax.fori_loop(max(bounds[i], 1), bounds[i + 1], up, state, unroll=3)
        low, high = levels - bounds[i + 1], levels - bounds[i]
        for f in range(4):
            copy = pltpu.make_async_copy(out.at[f, low:high], results[f].at[low:high], sem.at[i, f])
            copy.start()
            copies.append(copy)
    for copy in copies:
        copy.wait()


def local(lon_n, lat_n, t, s, u, v, mix, h):
    levels, height, width = t.shape
    padded = (levels + 7) // 8 * 8
    vmem = pl.BlockSpec(memory_space=pltpu.VMEM)
    hbm = pl.BlockSpec(memory_space=pltpu.HBM)
    field = jax.ShapeDtypeStruct((levels, height, width), F32)
    dma = pltpu.SemaphoreType.DMA
    swept = pl.pallas_call(
        functools.partial(forward_kernel, lon_n, lat_n),
        out_shape=(field,) * 5,
        in_specs=[hbm] * 6,
        out_specs=(vmem,) * 5,
        scratch_shapes=[
            pltpu.VMEM((4, levels, height, width), F32),
            pltpu.VMEM((levels - 1, height, width), F32),
            pltpu.VMEM((height, width), jnp.int32),
            pltpu.VMEM((height, width), F32),
            pltpu.VMEM((2, height, width), F32),
            pltpu.VMEM((2, 4, padded, width), F32),
            pltpu.VMEM((2, 4, padded, width), F32),
            pltpu.VMEM((2, 4, height, width), F32),
            pltpu.VMEM((2, 4, height, width), F32),
            pltpu.VMEM((2, height, width), F32),
            pltpu.VMEM((5, padded, width), F32),
            pltpu.VMEM((5, padded, width), F32),
            dma((6,)), dma((2,)), dma((2,)), dma((2, 3)), dma((2, 3)),
            dma((2,)), dma((2,)), dma((2,)), dma((2,)), dma,
        ],
        compiler_params=pltpu.CompilerParams(
            collective_id=0, has_side_effects=True, vmem_limit_bytes=24 << 20),
    )(t, s, u, v, mix, h)
    return pl.pallas_call(
        backward_kernel,
        out_shape=(field,) * 4,
        in_specs=[vmem] * 5,
        out_specs=(hbm,) * 4,
        scratch_shapes=[pltpu.VMEM((4, levels, height, width), F32), dma((4, 4))],
        compiler_params=pltpu.CompilerParams(vmem_limit_bytes=16 << 20),
    )(*swept)


def solution(mesh):
    field = P(None, "lat", "lon")
    return jax.shard_map(
        functools.partial(local, mesh.shape["lon"], mesh.shape["lat"]),
        mesh=mesh,
        in_specs=(field,) * 5 + (P("lat", "lon"),),
        out_specs=(field,) * 4,
        check_vma=False,
    )
```

```python
import functools

import numpy as np
import jax
import jax.numpy as jnp
from jax import lax
from jax.experimental import pallas as pl
from jax.experimental.pallas import tpu as pltpu
from jax.sharding import PartitionSpec as P

MESH = pl.DeviceIdType.MESH
F32 = jnp.float32

time_step = 0.2
coriolis_coef = 1.5
pressure_coef = 0.05


def face_tables(levels):
    part = time_step * 0.5
    ahead, last, factor = [], [], [0.0]
    for k in range(levels):
        above = part * (1.0 - factor[k]) if k else 0.0
        ahead.append(1.0 / (1.0 + part + above))
        last.append(1.0 / (1.0 + above))
        factor.append(part * ahead[k])
    return [np.asarray(x, np.float32) for x in (ahead, last, factor)]


def at_level(table, k):
    steady = table[-1]
    value = jnp.float32(float(steady))
    for i in range(len(table)):
        if table[i] != steady:
            value = jnp.where(k == i, jnp.float32(float(table[i])), value)
    return value


def chunks(levels, padded):
    return [(0, padded, levels)]


def forward_kernel(lon_n, lat_n, t_hbm, s_hbm, u_hbm, v_hbm, mix_hbm, h_hbm,
                   to_ref, so_ref, uo_ref, vo_ref, w_ref,
                   fields, mix, deep, deep_send, deep_got, row_send, rows, col_send, cols, corners,
                   north_ref, south_ref,
                   in_sem, deep_ss, deep_rs, row_ss, row_rs, col_ss, col_rs, cor_ss, cor_rs, fold_ss):
    levels, height, width = t_hbm.shape
    padded = rows.shape[2]
    parts = chunks(levels, padded)
    lon = lax.axis_index("lon")
    lat = lax.axis_index("lat")
    east = lax.rem(lon + 1, lon_n)
    west = lax.rem(lon + lon_n - 1, lon_n)
    mirror = lon_n - 1 - lon
    second = lax.rem(2 * lon_n - 2 - lon, lon_n)
    top = lat == lat_n - 1
    inner = jnp.logical_not(top)
    has_south = lat > 0
    far = jnp.logical_and(top, second != lon)

    loads = [pltpu.make_async_copy(src, dst, in_sem.at[i]) for i, (src, dst) in enumerate([
        (h_hbm, deep), (t_hbm, fields.at[0]), (s_hbm, fields.at[1]),
        (u_hbm, fields.at[2]), (v_hbm, fields.at[3]), (mix_hbm, mix)])]
    for load in loads:
        load.start()

    barrier = pltpu.get_barrier_semaphore()

    def greet(lon_to, lat_to):
        pl.semaphore_signal(barrier, inc=1, device_id={"lon": lon_to, "lat": lat_to}, device_id_type=MESH)

    @pl.when(top)
    def _():
        greet(mirror, lat)

    @pl.when(far)
    def _():
        greet(second, lat)

    greet(east, lat)
    greet(west, lat)

    @pl.when(has_south)
    def _():
        greet(lon, lat - 1)
        greet(east, lat - 1)

    @pl.when(inner)
    def _():
        greet(lon, lat + 1)
        greet(west, lat + 1)

    def remote(src, dst, send_sem, recv_sem, lon_to, lat_to):
        return pltpu.make_async_remote_copy(
            src_ref=src, dst_ref=dst, send_sem=send_sem, recv_sem=recv_sem,
            device_id={"lon": lon_to, "lat": lat_to}, device_id_type=MESH)

    def row_copy(c, own, slot, lon_to, lat_to):
        return remote(row_send.at[own, c], rows.at[slot, c], row_ss.at[own, c], row_rs.at[slot, c], lon_to, lat_to)

    to_north = [row_copy(c, 1, 1, lon, lat + 1) for c in range(4)]
    to_mirror = [row_copy(c, 1, 0, mirror, lat) for c in range(4)]
    to_south = [row_copy(c, 0, 0, lon, lat - 1) for c in range(4)]
    to_north.append(remote(deep_send, deep_got.at[1], deep_ss.at[1], deep_rs.at[1], lon, lat + 1))
    to_mirror.append(remote(deep_send, deep_got.at[0], deep_ss.at[1], deep_rs.at[0], mirror, lat))
    to_south.append(remote(deep_send, deep_got.at[0], deep_ss.at[0], deep_rs.at[0], lon, lat - 1))
    to_east = remote(col_send.at[0], cols.at[0], col_ss.at[0], col_rs.at[0], east, lat)
    to_west = remote(col_send.at[1], cols.at[1], col_ss.at[1], col_rs.at[1], west, lat)
    to_south_east = remote(col_send.at[0, 2], corners.at[0], cor_ss.at[0], cor_rs.at[0], east, lat - 1)
    to_north_west = remote(col_send.at[1, 3], corners.at[1], cor_ss.at[1], cor_rs.at[1], west, lat + 1)
    to_second = remote(col_send.at[0, 2], corners.at[0], fold_ss, cor_rs.at[0], second, lat)

    def send_rows(pieces):
        @pl.when(top)
        def _():
            for c in pieces:
                to_mirror[c].start()

        @pl.when(inner)
        def _():
            for c in pieces:
                to_north[c].start()

        @pl.when(has_south)
        def _():
            for c in pieces:
                to_south[c].start()

    loads[0].wait()
    depth = deep[...].astype(F32)
    deep_send[...] = depth
    peers = (2 + 2 * has_south.astype(jnp.int32) + 2 * inner.astype(jnp.int32)
             + top.astype(jnp.int32) + far.astype(jnp.int32))
    pl.semaphore_wait(barrier, peers)
    send_rows([4])
    for f in range(4):
        loads[1 + f].wait()
        row_send[0, f, :levels, :] = fields[f, :, 0, :]
        row_send[1, f, :levels, :] = fields[f, :, height - 1, :]
        send_rows([f])


    lane = lax.broadcasted_iota(jnp.int32, (height, width), 1)
    row = lax.broadcasted_iota(jnp.int32, (height, width), 0)
    zero = jnp.zeros((height, width), F32)

    def pack(k, packs):
        here, after = lane == k, lane == k + 1
        out = []
        for f in range(4):
            moved = pltpu.roll(fields[f, k], k + 1, 1)
            out.append(jnp.where(here, moved, packs[2 * f]))
            out.append(jnp.where(after, moved, packs[2 * f + 1]))
        return tuple(out)

    packs = lax.fori_loop(0, levels, pack, (zero,) * 8, unroll=5)
    for f in range(4):
        for side in range(2):
            tile = packs[2 * f + side]
            if f == 0:
                tile = jnp.where(lane == levels + side, pltpu.roll(depth, levels + 1, 1), tile)
            col_send[side, f] = tile

    to_east.start()
    to_west.start()

    @pl.when(far)
    def _():
        to_second.start()

    @pl.when(jnp.logical_and(top, second == lon))
    def _():
        corners[0] = col_send[0, 2]

    @pl.when(inner)
    def _():
        to_north_west.start()

    @pl.when(has_south)
    def _():
        to_south_east.start()


    first_lane, last_lane = lane == 0, lane == width - 1
    first_row, last_row = row == 0, row == height - 1

    def lanes(x, index):
        return jnp.take_along_axis(x, index, axis=1)

    def turned(x):
        wide = lax.broadcasted_iota(jnp.int32, x.shape, 1)
        return lanes(x, jnp.where(top, width - 1 - wide, wide))

    sign = jnp.where(top, -1.0, 1.0).astype(F32)
    loads[5].wait()
    to_east.wait()
    to_west.wait()

    @pl.when(inner)
    def _():
        to_south_east.wait_recv()
        to_north_west.wait_send()

    @pl.when(has_south)
    def _():
        to_north_west.wait_recv()
        to_south_east.wait_send()
        to_north[4].wait_recv()

    @pl.when(far)
    def _():
        to_second.wait()

    to_south[4].wait_recv()
    north_deep = turned(jnp.where(top, pltpu.roll(deep_got[0], 1, 0), deep_got[0]))[:1]
    south_deep = jnp.where(has_south, deep_got[1], 0.0)[height - 1 :]
    north_corner = jnp.where(top, corners[0, height - 1 :, :], corners[0, :1, :])
    north_corner = jnp.transpose(jnp.broadcast_to(north_corner, (width, width)))[:padded]
    south_corner = jnp.transpose(jnp.broadcast_to(pltpu.roll(corners[1], width - 1, 1)[height - 1 :], (width, width)))[:padded]

    def take_rows(c):
        a, b, _ = parts[c]
        for i in range(4):
            to_south[i].wait_recv()

        @pl.when(has_south)
        def _():
            for i in range(4):
                to_north[i].wait_recv()

        wide_lane = lax.broadcasted_iota(jnp.int32, (b - a, width), 1)
        corner = north_corner[a:b]
        north_ref[0, a:b] = turned(rows[0, 0, a:b])
        north_ref[1, a:b] = turned(rows[0, 1, a:b])
        zonal = turned(rows[0, 2, a:b])
        left = pltpu.roll(zonal, width - 1, 1)
        right = pltpu.roll(zonal, 1, 1)
        here = jnp.where(top, jnp.where(wide_lane == width - 1, corner, left), zonal)
        behind = jnp.where(top, zonal, jnp.where(wide_lane == 0, corner, right))
        north_ref[2, a:b] = sign * here
        north_ref[3, a:b] = sign * turned(rows[0, 3, a:b])
        north_ref[4, a:b] = sign * (here + behind)
        merid = rows[1, 3, a:b]
        for f in range(4):
            south_ref[f, a:b] = jnp.where(has_south, rows[1, f, a:b], 0.0)
        ahead = jnp.where(wide_lane == width - 1, south_corner[a:b], pltpu.roll(merid, width - 1, 1))
        south_ref[4, a:b] = jnp.where(has_south, merid + ahead, 0.0)

    def to_east_of(x, f, k):
        return jnp.where(last_lane, pltpu.roll(cols[1, f], width - 2 - k, 1), pltpu.roll(x, width - 1, 1))

    def to_west_of(x, f, k):
        return jnp.where(first_lane, pltpu.roll(cols[0, f], lax.rem(width - k, width), 1), pltpu.roll(x, 1, 1))

    def to_north_of(x, f, k):
        return jnp.where(last_row, north_ref[f, pl.ds(k, 1), :], pltpu.roll(x, height - 1, 0))

    def to_south_of(x, f, k):
        return jnp.where(first_row, south_ref[f, pl.ds(k, 1), :], pltpu.roll(x, 1, 0))

    east_depth = jnp.minimum(depth, to_east_of(depth, 0, levels))
    west_depth = jnp.minimum(depth, to_west_of(depth, 0, levels))
    north_depth = jnp.minimum(depth, jnp.where(last_row, north_deep, pltpu.roll(depth, height - 1, 0)))
    south_depth = jnp.minimum(depth, jnp.where(first_row, south_deep, pltpu.roll(depth, 1, 0)))

    centre = (lat * height + row).astype(F32) + 0.5
    coriolis = coriolis_coef * (2.0 * centre / (height * lat_n) - 1.0)
    spin = (0.25 * time_step) * coriolis
    tables = face_tables(levels)
    push = time_step * pressure_coef
    part = time_step * 0.5

    def density(t, s):
        return 0.8 * s - t * (1.0 + 0.1 * (t + s))

    def down(k, carry):
        heat, salt, zonal, merid, a, w, east_sum, north_sum = carry
        level = k.astype(F32) + 0.5
        t, s, u, v = fields[0, k], fields[1, k], fields[2, k], fields[3, k]
        te, tw, tn, ts = to_east_of(t, 0, k), to_west_of(t, 0, k), to_north_of(t, 0, k), to_south_of(t, 0, k)
        se, sw, sn, ss = to_east_of(s, 1, k), to_west_of(s, 1, k), to_north_of(s, 1, k), to_south_of(s, 1, k)
        ue, uw, un, us = to_east_of(u, 2, k), to_west_of(u, 2, k), to_north_of(u, 2, k), to_south_of(u, 2, k)
        ve, vw, vn, vs = to_east_of(v, 3, k), to_west_of(v, 3, k), to_north_of(v, 3, k), to_south_of(v, 3, k)
        uu, vv = u + uw, v + ve
        ubar = uu + to_north_of(uu, 4, k)
        vbar = vv + to_south_of(vv, 4, k)
        open_c = level < depth
        open_e, open_w = level < east_depth, level < west_depth
        open_n, open_s = level < north_depth, level < south_depth

        def face(mask, speed):
            x = part * speed
            return jnp.where(mask, part - x, 0.0), jnp.where(mask, part + x, 0.0)

        e_far, e_own = face(open_e, u)
        w_own, w_far = face(open_w, uw)
        n_far, n_own = face(open_n, v)
        s_own, s_far = face(open_s, vs)
        own = 1.0 - e_own - w_own - n_own - s_own
        t_star = own * t + e_far * te + w_far * tw + n_far * tn + s_far * ts
        s_star = own * s + e_far * se + w_far * sw + n_far * sn + s_far * ss

        rho = density(t, s)
        east_step = density(te, se) - rho
        north_step = density(tn, sn) - rho
        half_e = push * 0.5 * east_step
        half_n = push * 0.5 * north_step
        east_push = east_sum + half_e
        north_push = north_sum + half_n
        u_star = (1.0 - 4.0 * part) * u + part * (ue + uw + un + us) + spin * vbar - east_push
        v_star = (1.0 - 4.0 * part) * v + part * (ve + vw + vn + vs) - spin * ubar - north_push

        below = jnp.minimum(k, levels - 2)
        a_next = jnp.where(level + 1.0 < depth, time_step * mix[below], 0.0)
        d = (1.0 + a_next + a) - a * w
        r = pl.reciprocal(d, approx=True)
        r = r * (2.0 - d * r)
        w_next = a_next * r
        heat = jnp.where(open_c, (t_star + a * heat) * r, 0.0)
        salt = jnp.where(open_c, (s_star + a * salt) * r, 0.0)
        r_ahead, r_last = at_level(tables[0], k), at_level(tables[1], k)
        r_e = jnp.where(level + 1.0 < east_depth, r_ahead, r_last)
        r_n = jnp.where(level + 1.0 < north_depth, r_ahead, r_last)
        zonal = jnp.where(open_e, (u_star + part * zonal) * r_e, 0.0)
        merid = jnp.where(open_n, (v_star + part * merid) * r_n, 0.0)
        to_ref[k] = heat
        so_ref[k] = salt
        uo_ref[k] = zonal
        vo_ref[k] = merid
        w_ref[k] = w_next
        return heat, salt, zonal, merid, a_next, w_next, east_push + half_e, north_push + half_n

    state = (zero,) * 8
    for c in range(len(parts)):
        take_rows(c)
        state = lax.fori_loop(parts[c][0], parts[c][2], down, state, unroll=3)

    @pl.when(top)
    def _():
        for copy in to_mirror:
            copy.wait_send()

    @pl.when(inner)
    def _():
        for copy in to_north:
            copy.wait_send()

    @pl.when(has_south)
    def _():
        for copy in to_south:
            copy.wait_send()


def backward_kernel(to_ref, so_ref, uo_ref, vo_ref, w_ref, t_hbm, s_hbm, u_hbm, v_hbm, out, sem):
    levels, height, width = to_ref.shape
    factors = face_tables(levels)[2][1:]
    results = (t_hbm, s_hbm, u_hbm, v_hbm)
    heat, salt, zonal, merid = (ref[levels - 1] for ref in (to_ref, so_ref, uo_ref, vo_ref))
    for f, x in enumerate((heat, salt, zonal, merid)):
        out[f, levels - 1] = x

    def up(i, carry):
        heat, salt, zonal, merid = carry
        k = levels - 1 - i
        w = w_ref[k]
        wc = at_level(factors, k)
        heat = to_ref[k] + w * heat
        salt = so_ref[k] + w * salt
        zonal = uo_ref[k] + wc * zonal
        merid = vo_ref[k] + wc * merid
        for f, x in enumerate((heat, salt, zonal, merid)):
            out[f, k] = x
        return heat, salt, zonal, merid

    state = (heat, salt, zonal, merid)
    pieces = 4
    bounds = [levels * i // pieces for i in range(pieces + 1)]
    copies = []
    for i in range(pieces):
        state = lax.fori_loop(max(bounds[i], 1), bounds[i + 1], up, state, unroll=3)
        low, high = levels - bounds[i + 1], levels - bounds[i]
        for f in range(4):
            copy = pltpu.make_async_copy(out.at[f, low:high], results[f].at[low:high], sem.at[i, f])
            copy.start()
            copies.append(copy)
    for copy in copies:
        copy.wait()


def local(lon_n, lat_n, t, s, u, v, mix, h):
    levels, height, width = t.shape
    padded = (levels + 7) // 8 * 8
    vmem = pl.BlockSpec(memory_space=pltpu.VMEM)
    hbm = pl.BlockSpec(memory_space=pltpu.HBM)
    field = jax.ShapeDtypeStruct((levels, height, width), F32)
    dma = pltpu.SemaphoreType.DMA
    t, s, u, v, mix, h = (pltpu.with_memory_space_constraint(x, pltpu.HBM) for x in (t, s, u, v, mix, h))
    swept = pl.pallas_call(
        functools.partial(forward_kernel, lon_n, lat_n),
        out_shape=(field,) * 5,
        in_specs=[hbm] * 6,
        out_specs=(vmem,) * 5,
        scratch_shapes=[
            pltpu.VMEM((4, levels, height, width), F32),
            pltpu.VMEM((levels - 1, height, width), F32),
            pltpu.VMEM((height, width), jnp.int32),
            pltpu.VMEM((height, width), F32),
            pltpu.VMEM((2, height, width), F32),
            pltpu.VMEM((2, 4, padded, width), F32),
            pltpu.VMEM((2, 4, padded, width), F32),
            pltpu.VMEM((2, 4, height, width), F32),
            pltpu.VMEM((2, 4, height, width), F32),
            pltpu.VMEM((2, height, width), F32),
            pltpu.VMEM((5, padded, width), F32),
            pltpu.VMEM((5, padded, width), F32),
            dma((6,)), dma((2,)), dma((2,)), dma((2, 4)), dma((2, 4)),
            dma((2,)), dma((2,)), dma((2,)), dma((2,)), dma,
        ],
        compiler_params=pltpu.CompilerParams(
            collective_id=0, has_side_effects=True, vmem_limit_bytes=24 << 20),
    )(t, s, u, v, mix, h)
    return pl.pallas_call(
        backward_kernel,
        out_shape=(field,) * 4,
        in_specs=[vmem] * 5,
        out_specs=(hbm,) * 4,
        scratch_shapes=[pltpu.VMEM((4, levels, height, width), F32), dma((4, 4))],
        compiler_params=pltpu.CompilerParams(vmem_limit_bytes=16 << 20),
    )(*swept)


def solution(mesh):
    field = P(None, "lat", "lon")
    return jax.shard_map(
        functools.partial(local, mesh.shape["lon"], mesh.shape["lat"]),
        mesh=mesh,
        in_specs=(field,) * 5 + (P("lat", "lon"),),
        out_specs=(field,) * 4,
        check_vma=False,
    )
```

```python
import functools

import numpy as np
import jax
import jax.numpy as jnp
from jax import lax
from jax.experimental import pallas as pl
from jax.experimental.pallas import tpu as pltpu
from jax.sharding import PartitionSpec as P

MESH = pl.DeviceIdType.MESH
F32 = jnp.float32

time_step = 0.2
coriolis_coef = 1.5
pressure_coef = 0.05


def face_tables(levels):
    part = time_step * 0.5
    ahead, last, factor = [], [], [0.0]
    for k in range(levels):
        above = part * (1.0 - factor[k]) if k else 0.0
        ahead.append(1.0 / (1.0 + part + above))
        last.append(1.0 / (1.0 + above))
        factor.append(part * ahead[k])
    return [np.asarray(x, np.float32) for x in (ahead, last, factor)]


def at_level(table, k):
    steady = table[-1]
    value = jnp.float32(float(steady))
    for i in range(len(table)):
        if table[i] != steady:
            value = jnp.where(k == i, jnp.float32(float(table[i])), value)
    return value


def forward_kernel(lon_n, lat_n, t_hbm, s_hbm, u_hbm, v_hbm, mix_hbm, h_hbm,
                   to_ref, so_ref, uo_ref, vo_ref, w_ref,
                   fields, mix, deep, deep_send, deep_got, row_send, rows, col_send, cols, corners,
                   north_ref, south_ref, above_ref, r_ref,
                   in_sem, deep_ss, deep_rs, row_ss, row_rs, col_ss, col_rs, cor_ss, cor_rs, fold_ss):
    levels, height, width = t_hbm.shape
    padded = rows.shape[2]
    lon = lax.axis_index("lon")
    lat = lax.axis_index("lat")
    east = lax.rem(lon + 1, lon_n)
    west = lax.rem(lon + lon_n - 1, lon_n)
    mirror = lon_n - 1 - lon
    second = lax.rem(2 * lon_n - 2 - lon, lon_n)
    top = lat == lat_n - 1
    inner = jnp.logical_not(top)
    has_south = lat > 0
    far = jnp.logical_and(top, second != lon)

    loads = [pltpu.make_async_copy(src, dst, in_sem.at[i]) for i, (src, dst) in enumerate([
        (h_hbm, deep), (t_hbm, fields.at[0]), (s_hbm, fields.at[1]),
        (u_hbm, fields.at[2]), (v_hbm, fields.at[3]), (mix_hbm, mix)])]
    for load in loads:
        load.start()

    barrier = pltpu.get_barrier_semaphore()

    def greet(lon_to, lat_to):
        pl.semaphore_signal(barrier, inc=1, device_id={"lon": lon_to, "lat": lat_to}, device_id_type=MESH)

    @pl.when(top)
    def _():
        greet(mirror, lat)

    @pl.when(far)
    def _():
        greet(second, lat)

    greet(east, lat)
    greet(west, lat)

    @pl.when(has_south)
    def _():
        greet(lon, lat - 1)
        greet(east, lat - 1)

    @pl.when(inner)
    def _():
        greet(lon, lat + 1)
        greet(west, lat + 1)

    def remote(src, dst, send_sem, recv_sem, lon_to, lat_to):
        return pltpu.make_async_remote_copy(
            src_ref=src, dst_ref=dst, send_sem=send_sem, recv_sem=recv_sem,
            device_id={"lon": lon_to, "lat": lat_to}, device_id_type=MESH)

    def row_copy(c, own, slot, lon_to, lat_to):
        return remote(row_send.at[own, c], rows.at[slot, c], row_ss.at[own, c], row_rs.at[slot, c], lon_to, lat_to)

    to_north = [row_copy(c, 1, 1, lon, lat + 1) for c in range(4)]
    to_mirror = [row_copy(c, 1, 0, mirror, lat) for c in range(4)]
    to_south = [row_copy(c, 0, 0, lon, lat - 1) for c in range(4)]
    to_north.append(remote(deep_send, deep_got.at[1], deep_ss.at[1], deep_rs.at[1], lon, lat + 1))
    to_mirror.append(remote(deep_send, deep_got.at[0], deep_ss.at[1], deep_rs.at[0], mirror, lat))
    to_south.append(remote(deep_send, deep_got.at[0], deep_ss.at[0], deep_rs.at[0], lon, lat - 1))
    to_east = remote(col_send.at[0], cols.at[0], col_ss.at[0], col_rs.at[0], east, lat)
    to_west = remote(col_send.at[1], cols.at[1], col_ss.at[1], col_rs.at[1], west, lat)
    to_south_east = remote(col_send.at[0, 2], corners.at[0], cor_ss.at[0], cor_rs.at[0], east, lat - 1)
    to_north_west = remote(col_send.at[1, 3], corners.at[1], cor_ss.at[1], cor_rs.at[1], west, lat + 1)
    to_second = remote(col_send.at[0, 2], corners.at[0], fold_ss, cor_rs.at[0], second, lat)

    def send_rows(pieces):
        @pl.when(top)
        def _():
            for c in pieces:
                to_mirror[c].start()

        @pl.when(inner)
        def _():
            for c in pieces:
                to_north[c].start()

        @pl.when(has_south)
        def _():
            for c in pieces:
                to_south[c].start()

    loads[0].wait()
    depth = deep[...].astype(F32)
    deep_send[...] = depth
    peers = (2 + 2 * has_south.astype(jnp.int32) + 2 * inner.astype(jnp.int32)
             + top.astype(jnp.int32) + far.astype(jnp.int32))
    pl.semaphore_wait(barrier, peers)
    send_rows([4])
    for f in range(4):
        loads[1 + f].wait()
        row_send[0, f, :levels, :] = fields[f, :, 0, :]
        row_send[1, f, :levels, :] = fields[f, :, height - 1, :]
        send_rows([f])


    lane = lax.broadcasted_iota(jnp.int32, (height, width), 1)
    row = lax.broadcasted_iota(jnp.int32, (height, width), 0)
    zero = jnp.zeros((height, width), F32)

    def pack(k, packs):
        here, after = lane == k, lane == k + 1
        out = []
        for f in range(4):
            moved = pltpu.roll(fields[f, k], k + 1, 1)
            out.append(jnp.where(here, moved, packs[2 * f]))
            out.append(jnp.where(after, moved, packs[2 * f + 1]))
        return tuple(out)

    packs = lax.fori_loop(0, levels, pack, (zero,) * 8, unroll=5)
    for f in range(4):
        for side in range(2):
            tile = packs[2 * f + side]
            if f == 0:
                tile = jnp.where(lane == levels + side, pltpu.roll(depth, levels + 1, 1), tile)
            col_send[side, f] = tile

    to_east.start()
    to_west.start()

    @pl.when(far)
    def _():
        to_second.start()

    @pl.when(jnp.logical_and(top, second == lon))
    def _():
        corners[0] = col_send[0, 2]

    @pl.when(inner)
    def _():
        to_north_west.start()

    @pl.when(has_south)
    def _():
        to_south_east.start()


    first_lane, last_lane = lane == 0, lane == width - 1
    first_row, last_row = row == 0, row == height - 1

    def lanes(x, index):
        return jnp.take_along_axis(x, index, axis=1)

    def turned(x):
        wide = lax.broadcasted_iota(jnp.int32, x.shape, 1)
        return lanes(x, jnp.where(top, width - 1 - wide, wide))

    sign = jnp.where(top, -1.0, 1.0).astype(F32)
    loads[5].wait()
    to_east.wait()
    to_west.wait()

    @pl.when(inner)
    def _():
        to_north_west.wait_send()

    @pl.when(has_south)
    def _():
        to_north_west.wait_recv()
        to_south_east.wait_send()
        to_north[4].wait_recv()

    to_south[4].wait_recv()
    north_deep = turned(jnp.where(top, pltpu.roll(deep_got[0], 1, 0), deep_got[0]))[:1]
    south_deep = jnp.where(has_south, deep_got[1], 0.0)[height - 1 :]
    south_corner = jnp.transpose(jnp.broadcast_to(pltpu.roll(corners[1], width - 1, 1)[height - 1 :], (width, width)))[:padded]

    a, b = 0, padded

    def take_south():
        @pl.when(has_south)
        def _():
            for i in range(4):
                to_north[i].wait_recv()

        wide_lane = lax.broadcasted_iota(jnp.int32, (b - a, width), 1)
        merid = rows[1, 3, a:b]
        for f in range(4):
            south_ref[f, a:b] = jnp.where(has_south, rows[1, f, a:b], 0.0)
        ahead = jnp.where(wide_lane == width - 1, south_corner[a:b], pltpu.roll(merid, width - 1, 1))
        south_ref[4, a:b] = jnp.where(has_south, merid + ahead, 0.0)

    def take_north():
        for i in range(4):
            to_south[i].wait_recv()

        @pl.when(inner)
        def _():
            to_south_east.wait_recv()

        @pl.when(far)
        def _():
            to_second.wait()

        north_corner = jnp.where(top, corners[0, height - 1 :, :], corners[0, :1, :])
        north_corner = jnp.transpose(jnp.broadcast_to(north_corner, (width, width)))[:padded]
        wide_lane = lax.broadcasted_iota(jnp.int32, (b - a, width), 1)
        corner = north_corner[a:b]
        north_ref[0, a:b] = turned(rows[0, 0, a:b])
        north_ref[1, a:b] = turned(rows[0, 1, a:b])
        zonal = turned(rows[0, 2, a:b])
        left = pltpu.roll(zonal, width - 1, 1)
        right = pltpu.roll(zonal, 1, 1)
        here = jnp.where(top, jnp.where(wide_lane == width - 1, corner, left), zonal)
        behind = jnp.where(top, zonal, jnp.where(wide_lane == 0, corner, right))
        north_ref[2, a:b] = sign * here
        north_ref[3, a:b] = sign * turned(rows[0, 3, a:b])
        north_ref[4, a:b] = sign * (here + behind)

    def to_east_of(x, f, k):
        return jnp.where(last_lane, pltpu.roll(cols[1, f], width - 2 - k, 1), pltpu.roll(x, width - 1, 1))

    def to_west_of(x, f, k):
        return jnp.where(first_lane, pltpu.roll(cols[0, f], lax.rem(width - k, width), 1), pltpu.roll(x, 1, 1))

    def to_north_of(x, f, k):
        return jnp.where(last_row, 0.0, pltpu.roll(x, height - 1, 0))

    def to_south_of(x, f, k):
        return jnp.where(first_row, south_ref[f, pl.ds(k, 1), :], pltpu.roll(x, 1, 0))

    east_depth = jnp.minimum(depth, to_east_of(depth, 0, levels))
    west_depth = jnp.minimum(depth, to_west_of(depth, 0, levels))
    north_depth = jnp.minimum(depth, jnp.where(last_row, north_deep, pltpu.roll(depth, height - 1, 0)))
    south_depth = jnp.minimum(depth, jnp.where(first_row, south_deep, pltpu.roll(depth, 1, 0)))

    centre = (lat * height + row).astype(F32) + 0.5
    coriolis = coriolis_coef * (2.0 * centre / (height * lat_n) - 1.0)
    spin = (0.25 * time_step) * coriolis
    tables = face_tables(levels)
    push = time_step * pressure_coef
    part = time_step * 0.5

    def density(t, s):
        return 0.8 * s - t * (1.0 + 0.1 * (t + s))

    def down(k, carry):
        a, w, east_sum, north_sum = carry
        level = k.astype(F32) + 0.5
        t, s, u, v = fields[0, k], fields[1, k], fields[2, k], fields[3, k]
        te, tw, tn, ts = to_east_of(t, 0, k), to_west_of(t, 0, k), to_north_of(t, 0, k), to_south_of(t, 0, k)
        se, sw, sn, ss = to_east_of(s, 1, k), to_west_of(s, 1, k), to_north_of(s, 1, k), to_south_of(s, 1, k)
        ue, uw, un, us = to_east_of(u, 2, k), to_west_of(u, 2, k), to_north_of(u, 2, k), to_south_of(u, 2, k)
        ve, vw, vn, vs = to_east_of(v, 3, k), to_west_of(v, 3, k), to_north_of(v, 3, k), to_south_of(v, 3, k)
        uu, vv = u + uw, v + ve
        ubar = uu + to_north_of(uu, 4, k)
        vbar = vv + to_south_of(vv, 4, k)
        open_c = level < depth
        open_e, open_w = level < east_depth, level < west_depth
        open_n, open_s = level < north_depth, level < south_depth

        def face(mask, speed):
            x = part * speed
            return jnp.where(mask, part - x, 0.0), jnp.where(mask, part + x, 0.0)

        e_far, e_own = face(open_e, u)
        w_own, w_far = face(open_w, uw)
        n_far, n_own = face(open_n, v)
        s_own, s_far = face(open_s, vs)
        own = 1.0 - e_own - w_own - n_own - s_own
        t_star = own * t + e_far * te + w_far * tw + n_far * tn + s_far * ts
        s_star = own * s + e_far * se + w_far * sw + n_far * sn + s_far * ss

        rho = density(t, s)
        east_step = density(te, se) - rho
        north_step = density(tn, sn) - rho
        half_e = push * 0.5 * east_step
        half_n = push * 0.5 * north_step
        east_push = east_sum + half_e
        north_push = north_sum + half_n
        u_star = (1.0 - 4.0 * part) * u + part * (ue + uw + un + us) + spin * vbar - east_push
        v_star = (1.0 - 4.0 * part) * v + part * (ve + vw + vn + vs) - spin * ubar - north_push

        below = jnp.minimum(k, levels - 2)
        a_next = jnp.where(level + 1.0 < depth, time_step * mix[below], 0.0)
        d = (1.0 + a_next + a) - a * w
        r = pl.reciprocal(d, approx=True)
        r = r * (2.0 - d * r)
        w_next = a_next * r
        to_ref[k] = t_star
        so_ref[k] = s_star
        uo_ref[k] = u_star
        vo_ref[k] = v_star
        w_ref[k] = w_next
        above_ref[k] = a
        r_ref[k] = jnp.where(open_c, r, 0.0)
        return a_next, w_next, east_push + half_e, north_push + half_n

    def solve(k, carry):
        heat, salt, zonal, merid, north_sum = carry
        level = k.astype(F32) + 0.5
        open_e, open_n = level < east_depth, level < north_depth
        tn, sn, un, vn, uq = (jnp.where(last_row, north_ref[f, pl.ds(k, 1), :], 0.0) for f in range(5))
        n_far = jnp.where(open_n, part - part * fields[3, k], 0.0)
        half = push * 0.5 * density(tn, sn)
        north_push = north_sum + half
        a, r = above_ref[k], r_ref[k]
        u_star = uo_ref[k] + part * un
        v_star = vo_ref[k] + part * vn - spin * uq - north_push
        r_ahead, r_last = at_level(tables[0], k), at_level(tables[1], k)
        r_e = jnp.where(level + 1.0 < east_depth, r_ahead, r_last)
        r_n = jnp.where(level + 1.0 < north_depth, r_ahead, r_last)
        heat = (to_ref[k] + n_far * tn + a * heat) * r
        salt = (so_ref[k] + n_far * sn + a * salt) * r
        zonal = jnp.where(open_e, (u_star + part * zonal) * r_e, 0.0)
        merid = jnp.where(open_n, (v_star + part * merid) * r_n, 0.0)
        to_ref[k] = heat
        so_ref[k] = salt
        uo_ref[k] = zonal
        vo_ref[k] = merid
        return heat, salt, zonal, merid, north_push + half

    take_south()
    lax.fori_loop(0, levels, down, (zero,) * 4, unroll=3)
    take_north()
    lax.fori_loop(0, levels, solve, (zero,) * 5, unroll=3)

    @pl.when(top)
    def _():
        for copy in to_mirror:
            copy.wait_send()

    @pl.when(inner)
    def _():
        for copy in to_north:
            copy.wait_send()

    @pl.when(has_south)
    def _():
        for copy in to_south:
            copy.wait_send()


def backward_kernel(to_ref, so_ref, uo_ref, vo_ref, w_ref, t_hbm, s_hbm, u_hbm, v_hbm, out, sem):
    levels, height, width = to_ref.shape
    factors = face_tables(levels)[2][1:]
    results = (t_hbm, s_hbm, u_hbm, v_hbm)
    heat, salt, zonal, merid = (ref[levels - 1] for ref in (to_ref, so_ref, uo_ref, vo_ref))
    for f, x in enumerate((heat, salt, zonal, merid)):
        out[f, levels - 1] = x

    def up(i, carry):
        heat, salt, zonal, merid = carry
        k = levels - 1 - i
        w = w_ref[k]
        wc = at_level(factors, k)
        heat = to_ref[k] + w * heat
        salt = so_ref[k] + w * salt
        zonal = uo_ref[k] + wc * zonal
        merid = vo_ref[k] + wc * merid
        for f, x in enumerate((heat, salt, zonal, merid)):
            out[f, k] = x
        return heat, salt, zonal, merid

    state = (heat, salt, zonal, merid)
    pieces = 4
    bounds = [levels * i // pieces for i in range(pieces + 1)]
    copies = []
    for i in range(pieces):
        state = lax.fori_loop(max(bounds[i], 1), bounds[i + 1], up, state, unroll=3)
        low, high = levels - bounds[i + 1], levels - bounds[i]
        for f in range(4):
            copy = pltpu.make_async_copy(out.at[f, low:high], results[f].at[low:high], sem.at[i, f])
            copy.start()
            copies.append(copy)
    for copy in copies:
        copy.wait()


def local(lon_n, lat_n, t, s, u, v, mix, h):
    levels, height, width = t.shape
    padded = (levels + 7) // 8 * 8
    vmem = pl.BlockSpec(memory_space=pltpu.VMEM)
    hbm = pl.BlockSpec(memory_space=pltpu.HBM)
    field = jax.ShapeDtypeStruct((levels, height, width), F32)
    dma = pltpu.SemaphoreType.DMA
    t, s, u, v, mix, h = (pltpu.with_memory_space_constraint(x, pltpu.HBM) for x in (t, s, u, v, mix, h))
    swept = pl.pallas_call(
        functools.partial(forward_kernel, lon_n, lat_n),
        out_shape=(field,) * 5,
        in_specs=[hbm] * 6,
        out_specs=(vmem,) * 5,
        scratch_shapes=[
            pltpu.VMEM((4, levels, height, width), F32),
            pltpu.VMEM((levels - 1, height, width), F32),
            pltpu.VMEM((height, width), jnp.int32),
            pltpu.VMEM((height, width), F32),
            pltpu.VMEM((2, height, width), F32),
            pltpu.VMEM((2, 4, padded, width), F32),
            pltpu.VMEM((2, 4, padded, width), F32),
            pltpu.VMEM((2, 4, height, width), F32),
            pltpu.VMEM((2, 4, height, width), F32),
            pltpu.VMEM((2, height, width), F32),
            pltpu.VMEM((5, padded, width), F32),
            pltpu.VMEM((5, padded, width), F32),
            pltpu.VMEM((levels, height, width), F32),
            pltpu.VMEM((levels, height, width), F32),
            dma((6,)), dma((2,)), dma((2,)), dma((2, 4)), dma((2, 4)),
            dma((2,)), dma((2,)), dma((2,)), dma((2,)), dma,
        ],
        compiler_params=pltpu.CompilerParams(
            collective_id=0, has_side_effects=True, vmem_limit_bytes=24 << 20),
    )(t, s, u, v, mix, h)
    return pl.pallas_call(
        backward_kernel,
        out_shape=(field,) * 4,
        in_specs=[vmem] * 5,
        out_specs=(hbm,) * 4,
        scratch_shapes=[pltpu.VMEM((4, levels, height, width), F32), dma((4, 4))],
        compiler_params=pltpu.CompilerParams(vmem_limit_bytes=16 << 20),
    )(*swept)


def solution(mesh):
    field = P(None, "lat", "lon")
    return jax.shard_map(
        functools.partial(local, mesh.shape["lon"], mesh.shape["lat"]),
        mesh=mesh,
        in_specs=(field,) * 5 + (P("lat", "lon"),),
        out_specs=(field,) * 4,
        check_vma=False,
    )
```
